1024 devices in a mesh: ep: 64 (over z, y), tp: 16 (over x, core).
Axes of the slice: x: 8, y: 8, z: 8, core: 2. Of those that a mesh axis runs over, the one named last changes fastest.
Arguments:
- tokens: bfloat16 [2048, 3200], P('ep', 'tp'), may hold values from -6 to 6
- grad_out: bfloat16 [2048, 3200], P('ep', 'tp'), may hold values from -6 to 6
- route_weight: float32 [2048], P('ep'), may hold values from 0.1 to 1
- routes: int32 [2048, 1], P('ep'), may hold values from 0 to 15, as said below
- gate_weight: bfloat16 [64, 2288, 3200], P('ep', 'tp'), may hold values from -0.109375 to 0.109375
- up_weight: bfloat16 [64, 2288, 3200], P('ep', 'tp'), may hold values from -0.109375 to 0.109375
- down_weight: bfloat16 [64, 2288, 3200], P('ep', 'tp'), may hold values from -0.0625 to 0.0625
Outputs:
- grad_in: bfloat16 [2048, 3200], P('ep', 'tp')
The draws below stay inside these ranges and needn't reach their ends.
Inputs may be any that keep to these rules, and one draw needn't show every extreme that they name: `routes`: each token names one expert. In every device's block of 32 tokens (aligned blocks along the token dimension) no expert is named more than 4 times, and one expert, the same for all blocks, is named exactly 4 times in every block.
All inputs are finite; a program needn't handle non-finite values.
Results may differ from the reference program's by a relative error of at most 0.0049.
Values may be sent and summed in bfloat16 or wider, within the bound.
A program may use at most 32 MiB of HBM per device.

```python
import math
import jax
import jax.numpy as jnp
from jax import lax

D = 3200
FF = 9152
GROUP = 4
TOK_EP = 32
EXPERTS = 16
CAP = 4
TOKENS = 2048
N_EP = 64


def draw_routes(key, part):
    key = jax.random.fold_in(key, 11)
    hot_key, block_key = jax.random.split(key)
    hot_expert = jax.random.randint(hot_key, (), 0, EXPERTS, dtype=jnp.int32)
    tickets = jnp.arange(CAP * (EXPERTS - 1), dtype=jnp.int32) // CAP

    def one_block(single_key):
        first_key, second_key = jax.random.split(single_key)
        shuffled = jax.random.permutation(first_key, tickets)
        remaining = shuffled[:TOK_EP - CAP]
        remaining = remaining + (remaining >= hot_expert).astype(jnp.int32)
        chosen = jnp.concatenate([jnp.full((CAP,), hot_expert, jnp.int32), remaining])
        shuffle_order = jax.random.permutation(second_key, TOK_EP)
        return chosen[shuffle_order]
    block_keys = jax.random.split(block_key, TOKENS // TOK_EP)
    return jax.vmap(one_block)(block_keys).reshape(TOKENS, 1).astype(jnp.int32)


def shard_levels(key, dims, cuts, low, largest):
    level = 1.0
    for dim, parts in cuts:
        steps = jax.random.uniform(jax.random.fold_in(jax.random.fold_in(key, 6), dim), (parts,), jnp.float32, low / len(cuts), largest / len(cuts))
        level = level * jnp.repeat(jnp.exp(steps), dims[dim] // parts).reshape((-1,) + (1,) * (len(dims) - 1 - dim))
    return level


def gaussian(own_key, extent, spread, reach, pieces=(), held_as=jnp.bfloat16):
    drawn = jax.random.normal(own_key, extent, jnp.float32) * spread
    if len(pieces) > 0:
        drawn = shard_levels(own_key, extent, pieces, -0.22, 0.18) * drawn
    return jnp.clip(drawn, min=-reach, max=reach).astype(held_as)


def setup_inputs(seed: int = 0) -> dict:
    streams_of = jax.random.split(jax.random.key(seed), 8)
    tokens = gaussian(streams_of[0], (TOKENS, D), 1.0, 6.0, ((0, 64), (1, 16)))
    grad_out = gaussian(streams_of[1], (TOKENS, D), 1.0, 6.0, ((0, 64), (1, 16)))
    route_weight = jnp.clip(jnp.exp(math.log(1.0) - 2.3025851 * jax.random.uniform(streams_of[2], (TOKENS,), jnp.float32) ** shard_levels(streams_of[2], (TOKENS,), ((0, 64),), -0.2, 0.2)), 0.1, 1.0)
    routes = draw_routes(jax.random.fold_in(streams_of[7], 71), 0)
    gate_weight = gaussian(streams_of[4], (N_EP, FF // GROUP, D), D ** -0.5, 0.109375, ((0, 64), (1, 16)))
    up_weight = gaussian(streams_of[5], (N_EP, FF // GROUP, D), D ** -0.5, 0.109375, ((0, 64), (1, 16)))
    down_weight = gaussian(streams_of[6], (N_EP, FF // GROUP, D), FF ** -0.5, 0.0625, ((0, 64), (1, 16)))
    return {"tokens": tokens, "grad_out": grad_out, "route_weight": route_weight, "routes": routes, "gate_weight": gate_weight, "up_weight": up_weight, "down_weight": down_weight}


def reference(tokens, grad_out, route_weight, routes, gate_weight, up_weight, down_weight):
    experts = N_EP // GROUP
    slot_count = N_EP * CAP
    expert_of = routes[:, 0].astype(jnp.int32)
    onehot = (expert_of[:, None] == jnp.arange(experts, dtype=jnp.int32)[None, :]).astype(jnp.int32)
    rank_inside = (jnp.sum(jnp.cumsum(onehot, axis=0) * onehot, axis=1) - 1).astype(jnp.int32)
    all_gate = gate_weight.reshape(experts, FF, D)
    all_up = up_weight.reshape(experts, FF, D)
    all_down = down_weight.reshape(experts, FF, D)
    contract = (((1,), (1,)), ((), ()))
    slot_index = jnp.arange(slot_count, dtype=jnp.int32)

    def per_expert(total_grad, expert_id):
        chosen = expert_of == expert_id
        placement = (chosen[None, :] & (rank_inside[None, :] == slot_index[:, None])).astype(jnp.bfloat16)
        rows_x = jnp.dot(placement, tokens, preferred_element_type=jnp.float32).astype(jnp.bfloat16)
        rows_dy = jnp.dot(placement, grad_out, preferred_element_type=jnp.float32).astype(jnp.bfloat16)
        w_gate = lax.dynamic_index_in_dim(all_gate, expert_id, 0, keepdims=False)
        w_up = lax.dynamic_index_in_dim(all_up, expert_id, 0, keepdims=False)
        w_down = lax.dynamic_index_in_dim(all_down, expert_id, 0, keepdims=False)
        gate_pre = lax.dot_general(rows_x, w_gate, contract, preferred_element_type=jnp.float32)
        up_pre = lax.dot_general(rows_x, w_up, contract, preferred_element_type=jnp.float32)
        hidden_grad = lax.dot_general(rows_dy, w_down, contract, preferred_element_type=jnp.float32)
        sigmoid_gate = jax.nn.sigmoid(gate_pre)
        up_grad = (hidden_grad * gate_pre * sigmoid_gate).astype(jnp.bfloat16)
        gate_grad = (hidden_grad * up_pre * sigmoid_gate * (1.0 + gate_pre * (1.0 - sigmoid_gate))).astype(jnp.bfloat16)
        returned = jnp.dot(gate_grad, w_gate, preferred_element_type=jnp.float32) + jnp.dot(up_grad, w_up, preferred_element_type=jnp.float32)
        picked = jnp.take(returned, jnp.clip(rank_inside, 0, slot_count - 1), axis=0)
        return total_grad + jnp.where(chosen[:, None], picked, jnp.zeros_like(picked)), None

    total_grad, _ = lax.scan(per_expert, jnp.zeros((TOKENS, D), jnp.float32), jnp.arange(experts, dtype=jnp.int32))
    return (route_weight[:, None] * total_grad).astype(jnp.bfloat16)
```

```python
import functools

import jax
import jax.numpy as jnp
from jax import lax
from jax.experimental import pallas as pl
from jax.experimental.pallas import tpu as pltpu
from jax.sharding import PartitionSpec as P

NZ = 8
NY = 8
NX = 8
HALF = 4
CAP = 4
LANES = 128
WIDE = 256
BF = jnp.bfloat16
F32 = jnp.float32
NN = (((1,), (0,)), ((), ()))
TN = (((0,), (0,)), ((), ()))


def iota(shape, dim):
    return lax.broadcasted_iota(jnp.int32, shape, dim)


def hops(half, way):
    return 4 if half == way else 3


def kernel(
    tok, grd, weight, routes, gate_hbm, up_hbm, down_hbm, out,
    w_gate, w_up, w_down, w_sem,
    z_out, z_in, y_out, y_in, acts, part, twin, chain_out, chain_in,
    back_out, back_in, last_out, last_in,
    zs, zr, ys, yr, gs, gr, bs, br, ps, pr, cs, cr, us, ur, vs, vr,
):
    ep = lax.axis_index("ep")
    tp = lax.axis_index("tp")
    z, y = ep // NY, ep % NY
    x, c = tp // 2, tp % 2
    h, yy = y // HALF, y % HALF
    feat = tok.shape[1]
    hid = w_gate.shape[1]
    rows = part.shape[3]
    chip = 2 * feat

    def at(zz, yv, xx, cc):
        return {"ep": zz * NY + yv, "tp": xx * 2 + cc}

    def remote(src, dst, send, recv, where):
        return pltpu.make_async_remote_copy(
            src_ref=src, dst_ref=dst, send_sem=send, recv_sem=recv,
            device_id=where, device_id_type=pl.DeviceIdType.MESH,
        )

    def y_of(i):
        hh = h if i < HALF else 1 - h
        return hh, (yy + i) % HALF

    loads = []
    for n, (src, dst) in enumerate(((gate_hbm, w_gate), (up_hbm, w_up), (down_hbm, w_down))):
        load = pltpu.make_async_copy(src, dst, w_sem.at[n])
        load.start()
        loads.append(load)

    barrier = pltpu.get_barrier_semaphore()
    greeted = [at((z + k) % NZ, y, x, c) for k in range(1, NZ)]
    for i in range(NY):
        hh, yv = y_of(i)
        if i > 0:
            greeted.append(at(z, hh * HALF + yv, x, c))
        greeted.append(at(z, hh * HALF + yv, x, 1 - c))
    greeted.append(at(z, y, (x + 1) % NX, c))
    greeted.append(at(z, y, (x + NX - 1) % NX, c))
    for where in greeted:
        pl.semaphore_signal(barrier, inc=1, device_id=where, device_id_type=pl.DeviceIdType.MESH)

    n_tok = tok.shape[0]
    n_slot = NZ * 2 * CAP
    row_i, col_i = iota((n_tok, n_tok), 0), iota((n_tok, n_tok), 1)
    diag = row_i == col_i

    def column(v):
        return jnp.sum(jnp.where(diag, v, 0.0), axis=1, keepdims=True)

    r_row = routes[...].astype(F32)
    r_col = column(jnp.broadcast_to(r_row, (n_tok, n_tok)))
    same = jnp.where((r_col == r_row) & (row_i < col_i), 1.0, 0.0)
    slot_row = r_row * CAP + jnp.sum(same, axis=0, keepdims=True)
    slot_col = column(jnp.broadcast_to(slot_row, (n_tok, n_tok)))
    w_col = column(jnp.broadcast_to(weight[...], (n_tok, n_tok)))
    p_row = iota((2 * n_slot, n_tok), 0)
    p_slot = ((p_row // (2 * CAP)) * CAP + p_row % CAP).astype(F32)
    p_arr = (p_row // CAP) % 2
    hit = p_slot == slot_row
    put_x = jnp.where(hit & (p_arr == 0), 1.0, 0.0).astype(BF)
    put_g = jnp.where(hit & (p_arr == 1), 1.0, 0.0).astype(BF)
    packed = lax.dot_general(put_x, tok[...], NN, preferred_element_type=F32)
    packed += lax.dot_general(put_g, grd[...], NN, preferred_element_type=F32)
    packed = jnp.concatenate([packed, jnp.zeros((2 * n_slot, WIDE - feat), F32)], axis=1)
    z_out[...] = packed.astype(BF).reshape(z_out.shape)

    pl.semaphore_wait(barrier, len(greeted))

    z_copies = []
    for k in range(1, NZ):
        zd = (z + k) % NZ
        copy = remote(z_out.at[zd], z_in.at[z], zs.at[k - 1], zr.at[k - 1], at(zd, y, x, c))
        copy.start()
        z_copies.append(copy)
    z_in[z] = z_out[z]
    for load in loads:
        load.wait()
    for copy in z_copies:
        copy.wait_recv()

    n_in = 2 * n_slot
    q_out, q_in = iota((n_in, n_in), 0), iota((n_in, n_in), 1)
    per = NZ * CAP
    want = ((q_out % per) // CAP) * (4 * CAP) + (q_out // per) * CAP + q_out % CAP
    perm = jnp.where(q_in == want, 1.0, 0.0).astype(BF)
    moved = lax.dot_general(perm, z_in[...].reshape(n_in, WIDE), NN, preferred_element_type=F32)
    y_out[...] = moved.astype(BF).reshape(y_out.shape)

    y_copies = {}
    for i in range(NY):
        hh, yv = y_of(i)
        for o in range(2):
            if i == 0 and o == 0:
                continue
            cc = (c + o) % 2
            copy = remote(
                y_out.at[hh, cc], y_in.at[c, (i // HALF) * HALF + yy],
                ys.at[i, o], yr.at[i, o], at(z, hh * HALF + yv, x, cc),
            )
            copy.start()
            y_copies[i, o] = copy
    y_in[c, yy] = y_out[h, c]

    right, left = (x + 1) % NX, (x + NX - 1) % NX
    g_copies, b_copies = {}, {}

    def piece(j, way, s):
        return (x + NX - s) % NX if way == 0 else (x + s) % NX

    def hand_over(j, n, p):
        copy = remote(
            acts.at[c, j, p], acts.at[c, j, p], bs.at[j, n], br.at[j, n], at(z, y, x, 1 - c)
        )
        copy.start()
        b_copies[j, n] = copy

    def forward(j, way, s):
        p = piece(j, way, s)
        copy = remote(
            acts.at[c, j, p], acts.at[c, j, p], gs.at[j, way, s], gr.at[j, way, s],
            at(z, y, right if way == 0 else left, c),
        )
        copy.start()
        g_copies[j, way, s] = copy

    def begin(j):
        for i in range(j * HALF, j * HALF + HALF):
            for o in range(2):
                if (i, o) in y_copies:
                    y_copies[i, o].wait_recv()
        halves = []
        for core in range(2):
            block = y_in[core, j * HALF:(j + 1) * HALF].reshape(LANES, WIDE)
            halves.append(block.astype(F32).T[:feat])
        acts[c, j, x] = jnp.concatenate(halves, axis=0).astype(BF)
        forward(j, 0, 0)
        forward(j, 1, 0)
        hand_over(j, 0, x)

    def arrive(j, s):
        for way in range(2):
            if s > hops(j, way):
                continue
            g_copies[j, way, s - 1].wait_recv()
            if s < hops(j, way):
                forward(j, way, s)
            hand_over(j, s if way == 0 else hops(j, 0) + s, piece(j, way, s))

    def compute(j):
        for n in range(NX):
            b_copies[j, n].wait_recv()
        xs = acts[0, j].reshape(NX * chip, LANES)
        dy = acts[1, j].reshape(NX * chip, LANES)
        gate = lax.dot_general(w_gate[0], xs, NN, preferred_element_type=F32)
        up = lax.dot_general(w_up[0], xs, NN, preferred_element_type=F32)
        down = lax.dot_general(w_down[0], dy, NN, preferred_element_type=F32)
        sig = 1.0 / (1.0 + jnp.exp(-gate))
        up_grad = (down * gate * sig).astype(BF)
        gate_grad = (down * up * sig * (1.0 + gate * (1.0 - sig))).astype(BF)
        res = lax.dot_general(w_gate[0], gate_grad, TN, preferred_element_type=F32)
        res += lax.dot_general(w_up[0], up_grad, TN, preferred_element_type=F32)
        fill = jnp.zeros((rows - feat, LANES), F32)
        for px in range(NX):
            for pc in range(2):
                lo = px * chip + pc * feat
                part[j, pc, px] = jnp.concatenate([res[lo:lo + feat], fill], axis=0).astype(BF)
        copy = remote(part.at[j, 1 - c], twin.at[j], ps.at[j], pr.at[j], at(z, y, x, 1 - c))
        copy.start()
        return copy

    def own(j, d):
        return part[j, c, d].astype(F32) + twin[j, d].astype(F32)

    c_copies = {}

    def link(j, way, t):
        n = hops(j, way)
        d = (x + n - t) % NX if way == 0 else (x + NX - n + t) % NX
        val = own(j, d)
        if t > 0:
            c_copies[j, way, t - 1].wait_recv()
            val += chain_in[j, way, t - 1].astype(F32)
        chain_out[j, way, t] = val.astype(BF)
        copy = remote(
            chain_out.at[j, way, t], chain_in.at[j, way, t], cs.at[j, way, t], cr.at[j, way, t],
            at(z, y, right if way == 0 else left, c),
        )
        copy.start()
        c_copies[j, way, t] = copy

    u_copies = {}

    def give_back(j):
        val = own(j, x)
        for way in range(2):
            n = hops(j, way)
            c_copies[j, way, n - 1].wait_recv()
            val += chain_in[j, way, n - 1].astype(F32)
        val = jnp.concatenate([val, jnp.zeros((WIDE - rows, LANES), F32)], axis=0)
        back_out[j] = val.T.astype(BF).reshape(back_out.shape[1:])
        for i in range(j * HALF, j * HALF + HALF):
            hh, yv = y_of(i)
            if i == 0:
                continue
            copy = remote(
                back_out.at[j, yv], back_in.at[j * HALF + yy], us.at[i], ur.at[i],
                at(z, hh * HALF + yv, x, c),
            )
            copy.start()
            u_copies[i] = copy
        if j == 0:
            back_in[yy] = back_out[0, yy]

    begin(0)
    begin(1)
    for s in range(1, 4):
        arrive(0, s)
        arrive(1, s)
    arrive(0, 4)
    arrive(1, 4)
    p_copies = [compute(0), compute(1)]
    for j in range(2):
        p_copies[j].wait_recv()
        link(j, 0, 0)
        link(j, 1, 0)
    for t in range(1, 4):
        for j in range(2):
            for way in range(2):
                if t < hops(j, way):
                    link(j, way, t)
    give_back(0)
    give_back(1)

    sums = []
    for j in range(2):
        for i in range(j * HALF, j * HALF + HALF):
            if i > 0:
                u_copies[i].wait_recv()
        total = back_in[j * HALF].astype(F32)
        for n in range(1, HALF):
            total += back_in[j * HALF + n].astype(F32)
        sums.append(total)
    both = jnp.concatenate(sums, axis=0)
    v_out, v_in = iota((n_slot, n_slot), 0), iota((n_slot, n_slot), 1)
    half = (v_out // CAP) % 2
    rel = (half + h) % 2
    src = rel * per + (v_out // (2 * CAP)) * CAP + v_out % CAP
    turn = jnp.where(v_in == src, 1.0, 0.0)
    last_out[...] = lax.dot_general(
        turn, both, NN, precision=lax.Precision.HIGHEST, preferred_element_type=F32
    ).reshape(last_out.shape)
    v_copies = []
    for k in range(1, NZ):
        zd = (z + k) % NZ
        copy = remote(last_out.at[zd], last_in.at[z], vs.at[k - 1], vr.at[k - 1], at(zd, y, x, c))
        copy.start()
        v_copies.append(copy)
    last_in[z] = last_out[z]
    pick = jnp.where(slot_col == iota((n_tok, n_slot), 1).astype(F32), 1.0, 0.0)
    for copy in v_copies:
        copy.wait_recv()
    got = lax.dot_general(
        pick, last_in[...].reshape(n_slot, WIDE), NN,
        precision=lax.Precision.HIGHEST, preferred_element_type=F32,
    )
    out[...] = (w_col * got[:, :feat]).astype(BF)

    for group in (z_copies, y_copies.values(), g_copies.values(), b_copies.values(), p_copies,
                  c_copies.values(), u_copies.values(), v_copies):
        for copy in group:
            copy.wait_send()


def per_device(tokens, grad_out, route_weight, routes, gate_weight, up_weight, down_weight):
    n_tok, feat = tokens.shape
    _, hid, width = gate_weight.shape
    rows = -(-feat // 16) * 16
    vmem = pl.BlockSpec(memory_space=pltpu.VMEM)
    hbm = pl.BlockSpec(memory_space=pl.ANY)
    dma = pltpu.SemaphoreType.DMA
    n_slot = NZ * 2 * CAP
    return pl.pallas_call(
        kernel,
        out_shape=jax.ShapeDtypeStruct((n_tok, feat), BF),
        in_specs=[vmem, vmem, vmem, vmem, hbm, hbm, hbm],
        out_specs=vmem,
        scratch_shapes=[
            pltpu.VMEM((1, hid, width), BF),
            pltpu.VMEM((1, hid, width), BF),
            pltpu.VMEM((1, hid, width), BF),
            dma((3,)),
            pltpu.VMEM((NZ, 4 * CAP, WIDE), BF),
            pltpu.VMEM((NZ, 4 * CAP, WIDE), BF),
            pltpu.VMEM((2, 2, NZ * CAP, WIDE), BF),
            pltpu.VMEM((2, NY, NZ * CAP, WIDE), BF),
            pltpu.VMEM((2, 2, NX, 2 * feat, LANES), BF),
            pltpu.VMEM((2, 2, NX, rows, LANES), BF),
            pltpu.VMEM((2, NX, rows, LANES), BF),
            pltpu.VMEM((2, 2, 4, rows, LANES), BF),
            pltpu.VMEM((2, 2, 4, rows, LANES), BF),
            pltpu.VMEM((2, HALF, NZ * CAP, WIDE), BF),
            pltpu.VMEM((NY, NZ * CAP, WIDE), BF),
            pltpu.VMEM((NZ, 2 * CAP, WIDE), F32),
            pltpu.VMEM((NZ, 2 * CAP, WIDE), F32),
            dma((NZ - 1,)), dma((NZ - 1,)),
            dma((NY, 2)), dma((NY, 2)),
            dma((2, 2, 4)), dma((2, 2, 4)),
            dma((2, NX)), dma((2, NX)),
            dma((2,)), dma((2,)),
            dma((2, 2, 4)), dma((2, 2, 4)),
            dma((NY,)), dma((NY,)),
            dma((NZ - 1,)), dma((NZ - 1,)),
        ],
        compiler_params=pltpu.CompilerParams(
            collective_id=0, has_side_effects=True, vmem_limit_bytes=40 * 1024 * 1024
        ),
    )(
        tokens, grad_out, route_weight.reshape(1, n_tok), routes.reshape(1, n_tok),
        gate_weight, up_weight, down_weight,
    )


def solution(mesh):
    return jax.shard_map(
        per_device,
        mesh=mesh,
        in_specs=(
            P("ep", "tp"),
            P("ep", "tp"),
            P("ep"),
            P("ep", None),
            P("ep", "tp", None),
            P("ep", "tp", None),
            P("ep", "tp", None),
        ),
        out_specs=P("ep", "tp"),
        check_vma=False,
    )
```

```python
import functools

import jax
import jax.numpy as jnp
from jax import lax
from jax.experimental import pallas as pl
from jax.experimental.pallas import tpu as pltpu
from jax.sharding import PartitionSpec as P

NZ = 8
NY = 8
NX = 8
HALF = 4
CAP = 4
LANES = 128
WIDE = 256
BF = jnp.bfloat16
F32 = jnp.float32
NN = (((1,), (0,)), ((), ()))
TN = (((0,), (0,)), ((), ()))


G_CUT = (208, 192)
C_CUT = (112, 96)
FAR = NX // 2
STEPS = 3
ORDER = ((0, FAR), (0, 3), (1, 3), (0, 2), (1, 2), (0, 1), (1, 1), (0, 0))


def iota(shape, dim):
    return lax.broadcasted_iota(jnp.int32, shape, dim)


def kernel(
    tok_hbm, grd_hbm, weight_hbm, routes_hbm, gate_hbm, up_hbm, down_hbm, out,
    tok, grd, weight, routes, w_gate, w_up, w_down, w_sem,
    t_gate, t_up, z_out, z_in, y_out, y_in, f_out, f_in, acts, keep, part, twin, chain_out, chain_in,
    back_out, back_in, far_out, far_in, sum_out, sum_in, last_out, last_in,
    zs, zr, ys, yr, fs, fr, ws, wr, gs, gr, bs, br, ps, pr, cs, cr, us, ur, ks, kr, es, er, vs, vr,
):
    ep = lax.axis_index("ep")
    tp = lax.axis_index("tp")
    z, y = ep // NY, ep % NY
    x, c = tp // 2, tp % 2
    h, yy = y // HALF, y % HALF
    feat = tok.shape[1]
    rows = part.shape[2]
    chip = 2 * feat

    def at(zz, yv, xx, cc):
        return {"ep": zz * NY + yv, "tp": xx * 2 + cc}

    started = []

    def remote(src, dst, send, recv, where):
        copy = pltpu.make_async_remote_copy(
            src_ref=src, dst_ref=dst, send_sem=send, recv_sem=recv,
            device_id=where, device_id_type=pl.DeviceIdType.MESH,
        )
        copy.start()
        started.append(copy)
        return copy

    def y_of(i):
        hh = h if i < HALF else 1 - h
        return hh, (yy + i) % HALF

    loads = []
    for n, (src, dst) in enumerate((
        (routes_hbm, routes), (tok_hbm, tok), (grd_hbm, grd), (weight_hbm, weight),
        (gate_hbm, w_gate), (up_hbm, w_up), (down_hbm, w_down),
    )):
        load = pltpu.make_async_copy(src, dst, w_sem.at[n])
        load.start()
        loads.append(load)

    barrier = pltpu.get_barrier_semaphore()
    greeted = [at((z + k) % NZ, y, x, c) for k in range(1, NZ)]
    for i in range(NY):
        hh, yv = y_of(i)
        if i > 0:
            greeted.append(at(z, hh * HALF + yv, x, c))
        greeted.append(at(z, hh * HALF + yv, x, 1 - c))
    greeted.append(at(z, y, (x + FAR) % NX, c))
    greeted.append(at(z, y, (x + 1) % NX, c))
    greeted.append(at(z, y, (x + NX - 1) % NX, c))
    for where in greeted:
        pl.semaphore_signal(barrier, inc=1, device_id=where, device_id_type=pl.DeviceIdType.MESH)

    for load in loads[:4]:
        load.wait()
    n_tok = tok.shape[0]
    n_slot = NZ * 2 * CAP
    row_i, col_i = iota((n_tok, n_tok), 0), iota((n_tok, n_tok), 1)
    diag = row_i == col_i

    def column(v):
        return jnp.sum(jnp.where(diag, v, 0.0), axis=1, keepdims=True)

    r_row = routes[...].astype(F32)
    r_col = column(jnp.broadcast_to(r_row, (n_tok, n_tok)))
    same = jnp.where((r_col == r_row) & (row_i < col_i), 1.0, 0.0)
    slot_row = r_row * CAP + jnp.sum(same, axis=0, keepdims=True)
    slot_col = column(jnp.broadcast_to(slot_row, (n_tok, n_tok)))
    w_col = column(jnp.broadcast_to(weight[...], (n_tok, n_tok)))
    p_row = iota((2 * n_slot, n_tok), 0)
    p_slot = ((p_row // (2 * CAP)) * CAP + p_row % CAP).astype(F32)
    p_arr = (p_row // CAP) % 2
    hit = p_slot == slot_row
    put_x = jnp.where(hit & (p_arr == 0), 1.0, 0.0).astype(BF)
    put_g = jnp.where(hit & (p_arr == 1), 1.0, 0.0).astype(BF)
    packed = lax.dot_general(put_x, tok[...], NN, preferred_element_type=F32)
    packed += lax.dot_general(put_g, grd[...], NN, preferred_element_type=F32)
    packed = jnp.concatenate([packed, jnp.zeros((2 * n_slot, WIDE - feat), F32)], axis=1)
    z_out[...] = packed.astype(BF).reshape(z_out.shape)

    pl.semaphore_wait(barrier, len(greeted))

    z_copies = []
    for k in range(1, NZ):
        zd = (z + k) % NZ
        copy = remote(z_out.at[zd], z_in.at[z], zs.at[k - 1], zr.at[k - 1], at(zd, y, x, c))
        z_copies.append(copy)
    z_in[z] = z_out[z]
    for load in loads[4:]:
        load.wait()
    hid = w_gate.shape[1]
    unit = jnp.where(iota((hid, hid), 0) == iota((hid, hid), 1), 1.0, 0.0).astype(BF)

    def transpose(src, dst):
        res = lax.dot_general(src[0], unit, TN, preferred_element_type=F32)
        dst[...] = res.astype(BF).reshape(dst.shape)

    transpose(w_gate, t_gate)
    for copy in z_copies:
        copy.wait_recv()

    n_in = 2 * n_slot
    q_out, q_in = iota((n_in, n_in), 0), iota((n_in, n_in), 1)
    per = NZ * CAP
    want = ((q_out % per) // CAP) * (4 * CAP) + (q_out // per) * CAP + q_out % CAP
    perm = jnp.where(q_in == want, 1.0, 0.0).astype(BF)
    moved = lax.dot_general(perm, z_in[...].reshape(n_in, WIDE), NN, preferred_element_type=F32)
    y_out[...] = moved.astype(BF).reshape(y_out.shape)

    def spread(src, dst, send, recv):
        copies = {}
        for i in range(NY):
            hh, yv = y_of(i)
            for o in range(2):
                if i == 0 and o == 0:
                    continue
                cc = (c + o) % 2
                copies[i, o] = remote(
                    src.at[hh, cc], dst.at[c, (i // HALF) * HALF + yy],
                    send.at[i, o], recv.at[i, o], at(z, hh * HALF + yv, x, cc),
                )
        dst[c, yy] = src[h, c]
        return copies

    opposite = (x + FAR) % NX
    f_copy = remote(y_out, f_out, fs.at[0], fr.at[0], at(z, y, opposite, c))
    y_copies = spread(y_out, y_in, ys, yr)
    transpose(w_up, t_up)

    right, left = (x + 1) % NX, (x + NX - 1) % NX
    g_copies, b_copies = {}, {}

    def target(way, dist):
        return (x + dist) % NX if way == 0 else (x + NX - dist) % NX

    def cut(parts, n):
        lo = sum(parts[:n])
        return pl.ds(lo, parts[n])

    def hand_over(j, n, p, m):
        rest = acts.at[c, j, p, cut(G_CUT, m)]
        b_copies[j, n, m] = remote(rest, rest, bs.at[j, n, m], br.at[j, n, m], at(z, y, x, 1 - c))

    def forward(j, way, s, m):
        piece = acts.at[c, j, target(1 - way, s), cut(G_CUT, m)]
        g_copies[j, way, s, m] = remote(
            piece, piece, gs.at[j, way, s, m], gr.at[j, way, s, m],
            at(z, y, right if way == 0 else left, c),
        )

    def prepare(j, copies, src, p):
        for i in range(j * HALF, j * HALF + HALF):
            for o in range(2):
                if (i, o) in copies:
                    copies[i, o].wait_recv()
        halves = []
        for core in range(2):
            block = src[core, j * HALF:(j + 1) * HALF].reshape(LANES, WIDE)
            halves.append(block.astype(F32).T[:feat])
        acts[c, j, p] = jnp.concatenate(halves, axis=0).astype(BF)

    def begin(j):
        for m in range(len(G_CUT)):
            forward(j, 0, 0, m)
            forward(j, 1, 0, m)
        for m in range(len(G_CUT)):
            hand_over(j, 0, x, m)

    def arrive(j, s):
        for m in range(len(G_CUT)):
            for way in range(2):
                g_copies[j, way, s - 1, m].wait_recv()
                if s < STEPS:
                    forward(j, way, s, m)
                hand_over(j, s if way == 0 else STEPS + s, target(1 - way, s), m)

    def multiply():
        for copy in b_copies.values():
            copy.wait_recv()

        def both(a):
            return jnp.concatenate([acts[a, j].reshape(NX * chip, LANES) for j in range(2)], axis=1)

        xs, dy = both(0), both(1)
        gate = lax.dot_general(w_gate[0], xs, NN, preferred_element_type=F32)
        up = lax.dot_general(w_up[0], xs, NN, preferred_element_type=F32)
        down = lax.dot_general(w_down[0], dy, NN, preferred_element_type=F32)
        sig = 1.0 / (1.0 + jnp.exp(-gate))
        up_grad = (down * gate * sig).astype(BF)
        gate_grad = (down * up * sig * (1.0 + gate * (1.0 - sig))).astype(BF)
        return gate_grad, up_grad

    p_copies = {}

    def partials(gate_grad, up_grad):
        fill = jnp.zeros((rows - feat, LANES), F32)
        for n, (way, dist) in enumerate(ORDER):
            d = target(way, dist)
            res = lax.dot_general(t_gate[d], gate_grad, NN, preferred_element_type=F32)
            res += lax.dot_general(t_up[d], up_grad, NN, preferred_element_type=F32)
            for j in range(2):
                here = res[:, j * LANES:(j + 1) * LANES]
                low = jnp.concatenate([here[:feat], fill], axis=0)
                high = jnp.concatenate([here[feat:], fill], axis=0)
                keep[d, j] = jnp.where(c == 0, low, high)
                part[d, j] = jnp.where(c == 0, high, low).astype(BF)
            p_copies[way, dist] = remote(
                part.at[d], twin.at[d], ps.at[n], pr.at[n], at(z, y, x, 1 - c)
            )

    met = set()

    def own(j, way, dist):
        key = (0, 0) if dist == 0 else (way, dist)
        if key not in met:
            met.add(key)
            p_copies[key].wait_recv()
        d = target(way, dist)
        return keep[d, j] + twin[d, j].astype(F32)

    c_copies = {}

    def link(j, way, t):
        val = own(j, way, STEPS - t)
        for m in range(len(C_CUT)):
            here = cut(C_CUT, m)
            lo, hi = sum(C_CUT[:m]), sum(C_CUT[:m + 1])
            send = val[lo:hi]
            if t > 0:
                c_copies[j, way, t - 1, m].wait_recv()
                send += chain_in[j, way, t - 1, lo:hi].astype(F32)
            chain_out[j, way, t, lo:hi] = send.astype(BF)
            c_copies[j, way, t, m] = remote(
                chain_out.at[j, way, t, here], chain_in.at[j, way, t, here],
                cs.at[j, way, t, m], cr.at[j, way, t, m],
                at(z, y, right if way == 0 else left, c),
            )

    def give_back(j, val, src, dst, send, recv, copies):
        val = jnp.concatenate([val, jnp.zeros((WIDE - rows, LANES), F32)], axis=0)
        src[j] = val.T.astype(BF).reshape(src.shape[1:])
        for i in range(j * HALF, j * HALF + HALF):
            hh, yv = y_of(i)
            if i == 0:
                continue
            copies[i] = remote(
                src.at[j, yv], dst.at[j * HALF + yy], send.at[i], recv.at[i],
                at(z, hh * HALF + yv, x, c),
            )
        if j == 0:
            dst[yy] = src[0, yy]

    def collect(src, copies):
        sums = []
        for j in range(2):
            for i in range(j * HALF, j * HALF + HALF):
                if i > 0:
                    copies[i].wait_recv()
            total = src[j * HALF].astype(F32)
            for n in range(1, HALF):
                total += src[j * HALF + n].astype(F32)
            sums.append(total)
        return jnp.concatenate(sums, axis=0)

    prepare(0, y_copies, y_in, x)
    begin(0)
    f_copy.wait_recv()
    f_copies = spread(f_out, f_in, ws, wr)
    prepare(1, y_copies, y_in, x)
    begin(1)
    for s in range(1, STEPS + 1):
        for j in range(2):
            arrive(j, s)
        if s == 2:
            for j in range(2):
                prepare(j, f_copies, f_in, opposite)
                for m in range(len(G_CUT)):
                    hand_over(j, NX - 1, opposite, m)
    partials(*multiply())
    k_copies = {}
    for j in range(2):
        give_back(j, own(j, 0, FAR), far_out, far_in, ks, kr, k_copies)
    for t in range(STEPS):
        for j in range(2):
            link(j, j, t)
            link(j, 1 - j, t)
    sum_out[...] = collect(far_in, k_copies).astype(BF)
    e_copy = remote(sum_out, sum_in, es.at[0], er.at[0], at(z, y, opposite, c))
    u_copies = {}
    for j in range(2):
        val = own(j, 0, 0)
        for way in range(2):
            for m in range(len(C_CUT)):
                c_copies[j, way, STEPS - 1, m].wait_recv()
            val += chain_in[j, way, STEPS - 1].astype(F32)
        give_back(j, val, back_out, back_in, us, ur, u_copies)
    both = collect(back_in, u_copies)
    e_copy.wait_recv()
    both += sum_in[...].astype(F32)

    v_out, v_in = iota((n_slot, n_slot), 0), iota((n_slot, n_slot), 1)
    half = (v_out // CAP) % 2
    rel = (half + h) % 2
    src = rel * per + (v_out // (2 * CAP)) * CAP + v_out % CAP
    turn = jnp.where(v_in == src, 1.0, 0.0)
    last_out[...] = lax.dot_general(
        turn, both, NN, precision=lax.Precision.HIGHEST, preferred_element_type=F32
    ).reshape(last_out.shape)
    v_copies = []
    for k in range(1, NZ):
        zd = (z + k) % NZ
        copy = remote(last_out.at[zd], last_in.at[z], vs.at[k - 1], vr.at[k - 1], at(zd, y, x, c))
        v_copies.append(copy)
    last_in[z] = last_out[z]
    pick = jnp.where(slot_col == iota((n_tok, n_slot), 1).astype(F32), 1.0, 0.0)
    for copy in v_copies:
        copy.wait_recv()
    got = lax.dot_general(
        pick, last_in[...].reshape(n_slot, WIDE), NN,
        precision=lax.Precision.HIGHEST, preferred_element_type=F32,
    )
    out[...] = (w_col * got[:, :feat]).astype(BF)

    for copy in started:
        copy.wait_send()


def per_device(tokens, grad_out, route_weight, routes, gate_weight, up_weight, down_weight):
    n_tok, feat = tokens.shape
    _, hid, width = gate_weight.shape
    rows = -(-feat // 16) * 16
    vmem = pl.BlockSpec(memory_space=pltpu.VMEM)
    hbm = pl.BlockSpec(memory_space=pl.ANY)
    dma = pltpu.SemaphoreType.DMA
    n_slot = NZ * 2 * CAP
    return pl.pallas_call(
        kernel,
        out_shape=jax.ShapeDtypeStruct((n_tok, feat), BF),
        in_specs=[hbm] * 7,
        out_specs=vmem,
        scratch_shapes=[
            pltpu.VMEM((n_tok, feat), BF),
            pltpu.VMEM((n_tok, feat), BF),
            pltpu.VMEM((1, n_tok), F32),
            pltpu.VMEM((1, n_tok), jnp.int32),
            pltpu.VMEM((1, hid, width), BF),
            pltpu.VMEM((1, hid, width), BF),
            pltpu.VMEM((1, hid, width), BF),
            dma((7,)),
            pltpu.VMEM((NX, 2 * feat, hid), BF),
            pltpu.VMEM((NX, 2 * feat, hid), BF),
            pltpu.VMEM((NZ, 4 * CAP, WIDE), BF),
            pltpu.VMEM((NZ, 4 * CAP, WIDE), BF),
            pltpu.VMEM((2, 2, NZ * CAP, WIDE), BF),
            pltpu.VMEM((2, NY, NZ * CAP, WIDE), BF),
            pltpu.VMEM((2, 2, NZ * CAP, WIDE), BF),
            pltpu.VMEM((2, NY, NZ * CAP, WIDE), BF),
            pltpu.VMEM((2, 2, NX, 2 * feat, LANES), BF),
            pltpu.VMEM((NX, 2, rows, LANES), F32),
            pltpu.VMEM((NX, 2, rows, LANES), BF),
            pltpu.VMEM((NX, 2, rows, LANES), BF),
            pltpu.VMEM((2, 2, STEPS, rows, LANES), BF),
            pltpu.VMEM((2, 2, STEPS, rows, LANES), BF),
            pltpu.VMEM((2, HALF, NZ * CAP, WIDE), BF),
            pltpu.VMEM((NY, NZ * CAP, WIDE), BF),
            pltpu.VMEM((2, HALF, NZ * CAP, WIDE), BF),
            pltpu.VMEM((NY, NZ * CAP, WIDE), BF),
            pltpu.VMEM((2 * NZ * CAP, WIDE), BF),
            pltpu.VMEM((2 * NZ * CAP, WIDE), BF),
            pltpu.VMEM((NZ, 2 * CAP, WIDE), F32),
            pltpu.VMEM((NZ, 2 * CAP, WIDE), F32),
            dma((NZ - 1,)), dma((NZ - 1,)),
            dma((NY, 2)), dma((NY, 2)),
            dma((1,)), dma((1,)),
            dma((NY, 2)), dma((NY, 2)),
            dma((2, 2, STEPS, 2)), dma((2, 2, STEPS, 2)),
            dma((2, NX, 2)), dma((2, NX, 2)),
            dma((NX,)), dma((NX,)),
            dma((2, 2, STEPS, 2)), dma((2, 2, STEPS, 2)),
            dma((NY,)), dma((NY,)),
            dma((NY,)), dma((NY,)),
            dma((1,)), dma((1,)),
            dma((NZ - 1,)), dma((NZ - 1,)),
        ],
        compiler_params=pltpu.CompilerParams(
            collective_id=0, has_side_effects=True, vmem_limit_bytes=60 * 1024 * 1024
        ),
    )(
        tokens, grad_out, route_weight.reshape(1, n_tok), routes.reshape(1, n_tok),
        gate_weight, up_weight, down_weight,
    )


def solution(mesh):
    return jax.shard_map(
        per_device,
        mesh=mesh,
        in_specs=(
            P("ep", "tp"),
            P("ep", "tp"),
            P("ep"),
            P("ep", None),
            P("ep", "tp", None),
            P("ep", "tp", None),
            P("ep", "tp", None),
        ),
        out_specs=P("ep", "tp"),
        check_vma=False,
    )
```

```python
import functools

import jax
import jax.numpy as jnp
from jax import lax
from jax.experimental import pallas as pl
from jax.experimental.pallas import tpu as pltpu
from jax.sharding import PartitionSpec as P

NZ = 8
NY = 8
NX = 8
HALF = 4
CAP = 4
LANES = 128
WIDE = 256
BF = jnp.bfloat16
F32 = jnp.float32
NN = (((1,), (0,)), ((), ()))
TN = (((0,), (0,)), ((), ()))


G_CUT = (208, 192)
C_CUT = (112, 96)
FAR = NX // 2
STEPS = 3
ORDER = ((0, 3), (1, 3), (0, FAR), (0, 2), (1, 2), (0, 1), (1, 1), (0, 0))


def iota(shape, dim):
    return lax.broadcasted_iota(jnp.int32, shape, dim)


def kernel(
    tok_hbm, grd_hbm, weight_hbm, routes_hbm, gate_hbm, up_hbm, down_hbm, out,
    tok, grd, weight, routes, w_gate, w_up, w_down, w_sem,
    t_gate, t_up, w_cut, pre, z_out, z_in, y_out, y_in, f_out, h_in, h_out, f_in, acts, keep, part, twin, chain_out, chain_in,
    back_out, back_in, far_out, far_in, sum_out, sum_in, last_out, last_in,
    zs, zr, ys, yr, fs, fr, hs, hr, ws, wr, gs, gr, bs, br, ps, pr, cs, cr, us, ur, ks, kr, es, er, vs, vr,
):
    ep = lax.axis_index("ep")
    tp = lax.axis_index("tp")
    z, y = ep // NY, ep % NY
    x, c = tp // 2, tp % 2
    h, yy = y // HALF, y % HALF
    feat = tok.shape[1]
    rows = part.shape[2]
    chip = 2 * feat

    def at(zz, yv, xx, cc):
        return {"ep": zz * NY + yv, "tp": xx * 2 + cc}

    started = []

    def remote(src, dst, send, recv, where):
        copy = pltpu.make_async_remote_copy(
            src_ref=src, dst_ref=dst, send_sem=send, recv_sem=recv,
            device_id=where, device_id_type=pl.DeviceIdType.MESH,
        )
        copy.start()
        started.append(copy)
        return copy

    def y_of(i):
        hh = h if i < HALF else 1 - h
        return hh, (yy + i) % HALF

    barrier = pltpu.get_barrier_semaphore()
    greeted = [at((z + k) % NZ, y, x, c) for k in range(1, NZ)]
    for i in range(NY):
        hh, yv = y_of(i)
        if i > 0:
            greeted.append(at(z, hh * HALF + yv, x, c))
        greeted.append(at(z, hh * HALF + yv, x, 1 - c))
    greeted.append(at(z, y, (x + FAR) % NX, c))
    greeted.append(at(z, y, (x + 1) % NX, c))
    greeted.append(at(z, y, (x + NX - 1) % NX, c))
    for where in greeted:
        pl.semaphore_signal(barrier, inc=1, device_id=where, device_id_type=pl.DeviceIdType.MESH)

    loads = []
    for n, (src, dst) in enumerate((
        (routes_hbm, routes), (tok_hbm, tok), (grd_hbm, grd), (weight_hbm, weight),
        (gate_hbm, w_gate), (up_hbm, w_up), (down_hbm, w_down),
    )):
        load = pltpu.make_async_copy(src, dst, w_sem.at[n])
        load.start()
        loads.append(load)

    for load in loads[:4]:
        load.wait()
    n_tok = tok.shape[0]
    n_slot = NZ * 2 * CAP
    row_i, col_i = iota((n_tok, n_tok), 0), iota((n_tok, n_tok), 1)
    diag = row_i == col_i

    def column(v):
        return jnp.sum(jnp.where(diag, v, 0.0), axis=1, keepdims=True)

    r_row = routes[...].astype(F32)
    r_col = column(jnp.broadcast_to(r_row, (n_tok, n_tok)))
    same = jnp.where((r_col == r_row) & (row_i < col_i), 1.0, 0.0)
    slot_row = r_row * CAP + jnp.sum(same, axis=0, keepdims=True)
    slot_col = column(jnp.broadcast_to(slot_row, (n_tok, n_tok)))
    w_col = column(jnp.broadcast_to(weight[...], (n_tok, n_tok)))
    p_row = iota((2 * n_slot, n_tok), 0)
    p_slot = ((p_row // (2 * CAP)) * CAP + p_row % CAP).astype(F32)
    p_arr = (p_row // CAP) % 2
    hit = p_slot == slot_row
    put_x = jnp.where(hit & (p_arr == 0), 1.0, 0.0).astype(BF)
    put_g = jnp.where(hit & (p_arr == 1), 1.0, 0.0).astype(BF)
    packed = lax.dot_general(put_x, tok[...], NN, preferred_element_type=F32)
    packed += lax.dot_general(put_g, grd[...], NN, preferred_element_type=F32)
    packed = jnp.concatenate([packed, jnp.zeros((2 * n_slot, WIDE - feat), F32)], axis=1)
    z_out[...] = packed.astype(BF).reshape(z_out.shape)

    pl.semaphore_wait(barrier, len(greeted))

    def to_z(src, dst, send, recv):
        copies = []
        for k in range(1, NZ):
            zd = (z + k) % NZ
            copies.append(
                remote(src.at[zd], dst.at[z], send.at[k - 1], recv.at[k - 1], at(zd, y, x, c))
            )
        dst[z] = src[z]
        return copies

    z_copies = to_z(z_out, z_in, zs, zr)
    opposite = (x + FAR) % NX
    f_copy = remote(z_out, f_out, fs.at[0], fr.at[0], at(z, y, opposite, c))
    for load in loads[4:]:
        load.wait()
    hid = w_gate.shape[1]
    unit = jnp.where(iota((hid, hid), 0) == iota((hid, hid), 1), 1.0, 0.0).astype(BF)

    def transpose(src, dst):
        res = lax.dot_general(src[0], unit, TN, preferred_element_type=F32)
        for p in range(NX):
            low = res[p * chip:p * chip + feat]
            high = res[p * chip + feat:(p + 1) * chip]
            dst[p, 0] = jnp.where(c == 0, low, high).astype(BF)
            dst[p, 1] = jnp.where(c == 0, high, low).astype(BF)

    def cut_up(n, src):
        for p in range(NX):
            w_cut[n, p] = src[0, :, p * chip:(p + 1) * chip]

    transpose(w_gate, t_gate)
    cut_up(0, w_gate)
    n_in = 2 * n_slot
    q_out, q_in = iota((n_in, n_in), 0), iota((n_in, n_in), 1)
    per = NZ * CAP
    want = ((q_out % per) // CAP) * (4 * CAP) + (q_out // per) * CAP + q_out % CAP
    perm = jnp.where(q_in == want, 1.0, 0.0).astype(BF)

    def regroup(copies, src, dst):
        for copy in copies:
            copy.wait_recv()
        moved = lax.dot_general(perm, src[...].reshape(n_in, WIDE), NN, preferred_element_type=F32)
        dst[...] = moved.astype(BF).reshape(dst.shape)

    regroup(z_copies, z_in, y_out)

    def spread(src, dst, send, recv):
        copies = {}
        for i in range(NY):
            hh, yv = y_of(i)
            for o in range(2):
                if i == 0 and o == 0:
                    continue
                cc = (c + o) % 2
                copies[i, o] = remote(
                    src.at[hh, cc], dst.at[c, (i // HALF) * HALF + yy],
                    send.at[i, o], recv.at[i, o], at(z, hh * HALF + yv, x, cc),
                )
        dst[c, yy] = src[h, c]
        return copies

    y_copies = spread(y_out, y_in, ys, yr)
    transpose(w_up, t_up)
    cut_up(1, w_up)
    cut_up(2, w_down)
    f_copy.wait_recv()
    h_copies = to_z(f_out, h_in, hs, hr)

    right, left = (x + 1) % NX, (x + NX - 1) % NX
    g_copies, b_copies = {}, {}

    def target(way, dist):
        return (x + dist) % NX if way == 0 else (x + NX - dist) % NX

    def cut(parts, n):
        lo = sum(parts[:n])
        return pl.ds(lo, parts[n])

    def hand_over(j, n, p, m):
        rest = acts.at[c, j, p, cut(G_CUT, m)]
        b_copies[j, n, m] = remote(rest, rest, bs.at[j, n, m], br.at[j, n, m], at(z, y, x, 1 - c))

    def forward(j, way, s, m):
        piece = acts.at[c, j, target(1 - way, s), cut(G_CUT, m)]
        g_copies[j, way, s, m] = remote(
            piece, piece, gs.at[j, way, s, m], gr.at[j, way, s, m],
            at(z, y, right if way == 0 else left, c),
        )

    def prepare(j, copies, src, p):
        for i in range(j * HALF, j * HALF + HALF):
            for o in range(2):
                if (i, o) in copies:
                    copies[i, o].wait_recv()
        halves = []
        for core in range(2):
            block = src[core, j * HALF:(j + 1) * HALF].reshape(LANES, WIDE)
            halves.append(block.astype(F32).T[:feat])
        acts[c, j, p] = jnp.concatenate(halves, axis=0).astype(BF)

    def begin(j):
        for m in range(len(G_CUT)):
            forward(j, 0, 0, m)
            forward(j, 1, 0, m)
        for m in range(len(G_CUT)):
            hand_over(j, 0, x, m)

    def arrive(j, s):
        for m in range(len(G_CUT)):
            for way in range(2):
                g_copies[j, way, s - 1, m].wait_recv()
                if s < STEPS:
                    forward(j, way, s, m)
                hand_over(j, s if way == 0 else STEPS + s, target(1 - way, s), m)

    def add_piece(n, p, first=False):
        for j in range(2):
            for m in range(len(G_CUT)):
                b_copies[j, n, m].wait_recv()
        for n, a in ((0, 0), (1, 0), (2, 1)):
            piece = jnp.concatenate([acts[a, 0, p], acts[a, 1, p]], axis=1)
            res = lax.dot_general(w_cut[n, p], piece, NN, preferred_element_type=F32)
            pre[n] = res if first else pre[n] + res

    def add_step(s):
        add_piece(s, target(1, s))
        add_piece(STEPS + s, target(0, s))

    def gradients():
        gate, up, down = pre[0], pre[1], pre[2]
        sig = 1.0 / (1.0 + jnp.exp(-gate))
        up_grad = (down * gate * sig).astype(BF)
        gate_grad = (down * up * sig * (1.0 + gate * (1.0 - sig))).astype(BF)
        return gate_grad, up_grad

    p_copies = {}

    def partials(gate_grad, up_grad):
        fill = jnp.zeros((rows - feat, LANES), F32)
        for n, (way, dist) in enumerate(ORDER):
            d = target(way, dist)
            for side in range(2):
                res = lax.dot_general(t_gate[d, side], gate_grad, NN, preferred_element_type=F32)
                res += lax.dot_general(t_up[d, side], up_grad, NN, preferred_element_type=F32)
                for j in range(2):
                    here = jnp.concatenate([res[:, j * LANES:(j + 1) * LANES], fill], axis=0)
                    if side == 0:
                        keep[d, j] = here
                    else:
                        part[d, j] = here.astype(BF)
            p_copies[way, dist] = remote(
                part.at[d], twin.at[d], ps.at[n], pr.at[n], at(z, y, x, 1 - c)
            )

    met = set()

    def own(j, way, dist):
        key = (0, 0) if dist == 0 else (way, dist)
        if key not in met:
            met.add(key)
            p_copies[key].wait_recv()
        d = target(way, dist)
        return keep[d, j] + twin[d, j].astype(F32)

    c_copies = {}

    def link(j, way, t):
        val = own(j, way, STEPS - t)
        for m in range(len(C_CUT)):
            here = cut(C_CUT, m)
            lo, hi = sum(C_CUT[:m]), sum(C_CUT[:m + 1])
            send = val[lo:hi]
            if t > 0:
                c_copies[j, way, t - 1, m].wait_recv()
                send += chain_in[j, way, t - 1, lo:hi].astype(F32)
            chain_out[j, way, t, lo:hi] = send.astype(BF)
            c_copies[j, way, t, m] = remote(
                chain_out.at[j, way, t, here], chain_in.at[j, way, t, here],
                cs.at[j, way, t, m], cr.at[j, way, t, m],
                at(z, y, right if way == 0 else left, c),
            )

    def give_back(j, val, src, dst, send, recv, copies):
        val = jnp.concatenate([val, jnp.zeros((WIDE - rows, LANES), F32)], axis=0)
        src[j] = val.T.astype(BF).reshape(src.shape[1:])
        for i in range(j * HALF, j * HALF + HALF):
            hh, yv = y_of(i)
            if i == 0:
                continue
            copies[i] = remote(
                src.at[j, yv], dst.at[j * HALF + yy], send.at[i], recv.at[i],
                at(z, hh * HALF + yv, x, c),
            )
        if j == 0:
            dst[yy] = src[0, yy]

    def collect(src, copies):
        sums = []
        for j in range(2):
            for i in range(j * HALF, j * HALF + HALF):
                if i > 0:
                    copies[i].wait_recv()
            total = src[j * HALF].astype(F32)
            for n in range(1, HALF):
                total += src[j * HALF + n].astype(F32)
            sums.append(total)
        return jnp.concatenate(sums, axis=0)

    for j in range(2):
        prepare(j, y_copies, y_in, x)
        begin(j)
    regroup(h_copies, h_in, h_out)
    f_copies = spread(h_out, f_in, ws, wr)
    for s in range(1, STEPS + 1):
        for j in range(2):
            arrive(j, s)
        if s == 1:
            add_piece(0, x, True)
        elif s == 2:
            add_step(1)
            for j in range(2):
                prepare(j, f_copies, f_in, opposite)
                for m in range(len(G_CUT)):
                    hand_over(j, NX - 1, opposite, m)
    add_step(2)
    add_piece(NX - 1, opposite)
    add_step(STEPS)
    partials(*gradients())
    k_copies = {}
    for t in range(STEPS):
        if t == 1:
            for j in (1, 0):
                give_back(j, own(j, 0, FAR), far_out, far_in, ks, kr, k_copies)
        for j in (1, 0):
            link(j, j, t)
            link(j, 1 - j, t)
    sum_out[...] = collect(far_in, k_copies).astype(BF)
    e_copy = remote(sum_out, sum_in, es.at[0], er.at[0], at(z, y, opposite, c))
    u_copies = {}
    for j in (1, 0):
        val = own(j, 0, 0)
        for way in range(2):
            for m in range(len(C_CUT)):
                c_copies[j, way, STEPS - 1, m].wait_recv()
            val += chain_in[j, way, STEPS - 1].astype(F32)
        give_back(j, val, back_out, back_in, us, ur, u_copies)
    both = collect(back_in, u_copies)
    e_copy.wait_recv()
    both += sum_in[...].astype(F32)

    v_out, v_in = iota((n_slot, n_slot), 0), iota((n_slot, n_slot), 1)
    half = (v_out // CAP) % 2
    rel = (half + h) % 2
    src = rel * per + (v_out // (2 * CAP)) * CAP + v_out % CAP
    turn = jnp.where(v_in == src, 1.0, 0.0)
    last_out[...] = lax.dot_general(
        turn, both, NN, precision=lax.Precision.HIGHEST, preferred_element_type=F32
    ).reshape(last_out.shape)
    v_copies = []
    for k in range(1, NZ):
        zd = (z + k) % NZ
        copy = remote(last_out.at[zd], last_in.at[z], vs.at[k - 1], vr.at[k - 1], at(zd, y, x, c))
        v_copies.append(copy)
    last_in[z] = last_out[z]
    pick = jnp.where(slot_col == iota((n_tok, n_slot), 1).astype(F32), 1.0, 0.0)
    for copy in v_copies:
        copy.wait_recv()
    got = lax.dot_general(
        pick, last_in[...].reshape(n_slot, WIDE), NN,
        precision=lax.Precision.HIGHEST, preferred_element_type=F32,
    )
    out[...] = (w_col * got[:, :feat]).astype(BF)

    for copy in started:
        copy.wait_send()


def per_device(tokens, grad_out, route_weight, routes, gate_weight, up_weight, down_weight):
    n_tok, feat = tokens.shape
    _, hid, width = gate_weight.shape
    rows = -(-feat // 16) * 16
    vmem = pl.BlockSpec(memory_space=pltpu.VMEM)
    hbm = pl.BlockSpec(memory_space=pl.ANY)
    dma = pltpu.SemaphoreType.DMA
    n_slot = NZ * 2 * CAP
    return pl.pallas_call(
        kernel,
        out_shape=jax.ShapeDtypeStruct((n_tok, feat), BF),
        in_specs=[hbm] * 7,
        out_specs=vmem,
        scratch_shapes=[
            pltpu.VMEM((n_tok, feat), BF),
            pltpu.VMEM((n_tok, feat), BF),
            pltpu.VMEM((1, n_tok), F32),
            pltpu.VMEM((1, n_tok), jnp.int32),
            pltpu.VMEM((1, hid, width), BF),
            pltpu.VMEM((1, hid, width), BF),
            pltpu.VMEM((1, hid, width), BF),
            dma((7,)),
            pltpu.VMEM((NX, 2, feat, hid), BF),
            pltpu.VMEM((NX, 2, feat, hid), BF),
            pltpu.VMEM((3, NX, hid, 2 * feat), BF),
            pltpu.VMEM((3, hid, 2 * LANES), F32),
            pltpu.VMEM((NZ, 4 * CAP, WIDE), BF),
            pltpu.VMEM((NZ, 4 * CAP, WIDE), BF),
            pltpu.VMEM((2, 2, NZ * CAP, WIDE), BF),
            pltpu.VMEM((2, NY, NZ * CAP, WIDE), BF),
            pltpu.VMEM((NZ, 4 * CAP, WIDE), BF),
            pltpu.VMEM((NZ, 4 * CAP, WIDE), BF),
            pltpu.VMEM((2, 2, NZ * CAP, WIDE), BF),
            pltpu.VMEM((2, NY, NZ * CAP, WIDE), BF),
            pltpu.VMEM((2, 2, NX, 2 * feat, LANES), BF),
            pltpu.VMEM((NX, 2, rows, LANES), F32),
            pltpu.VMEM((NX, 2, rows, LANES), BF),
            pltpu.VMEM((NX, 2, rows, LANES), BF),
            pltpu.VMEM((2, 2, STEPS, rows, LANES), BF),
            pltpu.VMEM((2, 2, STEPS, rows, LANES), BF),
            pltpu.VMEM((2, HALF, NZ * CAP, WIDE), BF),
            pltpu.VMEM((NY, NZ * CAP, WIDE), BF),
            pltpu.VMEM((2, HALF, NZ * CAP, WIDE), BF),
            pltpu.VMEM((NY, NZ * CAP, WIDE), BF),
            pltpu.VMEM((2 * NZ * CAP, WIDE), BF),
            pltpu.VMEM((2 * NZ * CAP, WIDE), BF),
            pltpu.VMEM((NZ, 2 * CAP, WIDE), F32),
            pltpu.VMEM((NZ, 2 * CAP, WIDE), F32),
            dma((NZ - 1,)), dma((NZ - 1,)),
            dma((NY, 2)), dma((NY, 2)),
            dma((1,)), dma((1,)),
            dma((NZ - 1,)), dma((NZ - 1,)),
            dma((NY, 2)), dma((NY, 2)),
            dma((2, 2, STEPS, 2)), dma((2, 2, STEPS, 2)),
            dma((2, NX, 2)), dma((2, NX, 2)),
            dma((NX,)), dma((NX,)),
            dma((2, 2, STEPS, 2)), dma((2, 2, STEPS, 2)),
            dma((NY,)), dma((NY,)),
            dma((NY,)), dma((NY,)),
            dma((1,)), dma((1,)),
            dma((NZ - 1,)), dma((NZ - 1,)),
        ],
        compiler_params=pltpu.CompilerParams(
            collective_id=0, has_side_effects=True, vmem_limit_bytes=60 * 1024 * 1024
        ),
    )(
        tokens, grad_out, route_weight.reshape(1, n_tok), routes.reshape(1, n_tok),
        gate_weight, up_weight, down_weight,
    )


def solution(mesh):
    return jax.shard_map(
        per_device,
        mesh=mesh,
        in_specs=(
            P("ep", "tp"),
            P("ep", "tp"),
            P("ep"),
            P("ep", None),
            P("ep", "tp", None),
            P("ep", "tp", None),
            P("ep", "tp", None),
        ),
        out_specs=P("ep", "tp"),
        check_vma=False,
    )
```

```python
import functools

import jax
import jax.numpy as jnp
from jax import lax
from jax.experimental import pallas as pl
from jax.experimental.pallas import tpu as pltpu
from jax.sharding import PartitionSpec as P

NZ = 8
NY = 8
NX = 8
HALF = 4
CAP = 4
LANES = 128
WIDE = 256
BF = jnp.bfloat16
F32 = jnp.float32
NN = (((1,), (0,)), ((), ()))
TN = (((0,), (0,)), ((), ()))


G_CUT = (208, 192)
C_CUT = (112, 96)
FAR = NX // 2
STEPS = 3
FARTHEST = (4, 3, 5, 2, 6, 1, 7)
ORDER = ((0, 3), (1, 3), (0, FAR), (0, 2), (1, 2), (0, 1), (1, 1), (0, 0))


def iota(shape, dim):
    return lax.broadcasted_iota(jnp.int32, shape, dim)


def kernel(
    tok_hbm, grd_hbm, weight_hbm, routes_hbm, gate_hbm, up_hbm, down_hbm, out,
    tok, grd, weight, routes, w_gate, w_up, w_down, w_sem,
    t_gate, t_up, w_cut, pre, z_out, z_in, y_out, y_in, f_out, h_in, h_out, f_in, acts, keep, part, twin, chain_out, chain_in,
    back_out, back_in, far_out, far_in, sum_out, sum_in, last_out, last_in,
    zs, zr, ys, yr, fs, fr, hs, hr, ws, wr, gs, gr, bs, br, ps, pr, cs, cr, us, ur, ks, kr, es, er, vs, vr,
):
    ep = lax.axis_index("ep")
    tp = lax.axis_index("tp")
    z, y = ep // NY, ep % NY
    x, c = tp // 2, tp % 2
    h, yy = y // HALF, y % HALF
    feat = tok.shape[1]
    rows = part.shape[2]
    chip = 2 * feat

    def at(zz, yv, xx, cc):
        return {"ep": zz * NY + yv, "tp": xx * 2 + cc}

    started = []

    def remote(src, dst, send, recv, where):
        copy = pltpu.make_async_remote_copy(
            src_ref=src, dst_ref=dst, send_sem=send, recv_sem=recv,
            device_id=where, device_id_type=pl.DeviceIdType.MESH,
        )
        copy.start()
        started.append(copy)
        return copy

    def drain(most=None):
        n = len(started) if most is None else most
        for copy in started[:n]:
            copy.wait_send()
        del started[:n]

    def y_of(i):
        hh = h if i < HALF else 1 - h
        return hh, (yy + i) % HALF

    barrier = pltpu.get_barrier_semaphore()
    greeted = [at((z + k) % NZ, y, x, c) for k in FARTHEST]
    for i in range(NY):
        hh, yv = y_of(i)
        if i > 0:
            greeted.append(at(z, hh * HALF + yv, x, c))
        greeted.append(at(z, hh * HALF + yv, x, 1 - c))
    greeted.append(at(z, y, (x + FAR) % NX, c))
    greeted.append(at(z, y, (x + 1) % NX, c))
    greeted.append(at(z, y, (x + NX - 1) % NX, c))
    for where in greeted:
        pl.semaphore_signal(barrier, inc=1, device_id=where, device_id_type=pl.DeviceIdType.MESH)

    loads = []
    for n, (src, dst) in enumerate((
        (routes_hbm, routes), (tok_hbm, tok), (grd_hbm, grd), (weight_hbm, weight),
        (gate_hbm, w_gate), (up_hbm, w_up), (down_hbm, w_down),
    )):
        load = pltpu.make_async_copy(src, dst, w_sem.at[n])
        load.start()
        loads.append(load)

    for load in loads[:4]:
        load.wait()
    n_tok = tok.shape[0]
    n_slot = NZ * 2 * CAP
    row_i, col_i = iota((n_tok, n_tok), 0), iota((n_tok, n_tok), 1)
    diag = row_i == col_i

    def column(v):
        return jnp.sum(jnp.where(diag, v, 0.0), axis=1, keepdims=True)

    r_row = routes[...].astype(F32)
    r_col = column(jnp.broadcast_to(r_row, (n_tok, n_tok)))
    same = jnp.where((r_col == r_row) & (row_i < col_i), 1.0, 0.0)
    slot_row = r_row * CAP + jnp.sum(same, axis=0, keepdims=True)
    slot_col = column(jnp.broadcast_to(slot_row, (n_tok, n_tok)))
    w_col = column(jnp.broadcast_to(weight[...], (n_tok, n_tok)))
    p_row = iota((2 * n_slot, n_tok), 0)
    p_slot = ((p_row // (2 * CAP)) * CAP + p_row % CAP).astype(F32)
    p_arr = (p_row // CAP) % 2
    hit = p_slot == slot_row
    put_x = jnp.where(hit & (p_arr == 0), 1.0, 0.0).astype(BF)
    put_g = jnp.where(hit & (p_arr == 1), 1.0, 0.0).astype(BF)
    packed = lax.dot_general(put_x, tok[...], NN, preferred_element_type=F32)
    packed += lax.dot_general(put_g, grd[...], NN, preferred_element_type=F32)
    packed = jnp.concatenate([packed, jnp.zeros((2 * n_slot, WIDE - feat), F32)], axis=1)
    z_out[...] = packed.astype(BF).reshape(z_out.shape)

    pl.semaphore_wait(barrier, len(greeted))

    def to_z(src, dst, send, recv):
        copies = []
        for k in FARTHEST:
            zd = (z + k) % NZ
            copies.append(
                remote(src.at[zd], dst.at[z], send.at[k - 1], recv.at[k - 1], at(zd, y, x, c))
            )
        dst[z] = src[z]
        return copies

    z_copies = to_z(z_out, z_in, zs, zr)
    opposite = (x + FAR) % NX
    f_copy = remote(z_out, f_out, fs.at[0], fr.at[0], at(z, y, opposite, c))
    for load in loads[4:]:
        load.wait()
    hid = w_gate.shape[1]
    unit = jnp.where(iota((hid, hid), 0) == iota((hid, hid), 1), 1.0, 0.0).astype(BF)

    def transpose(src, dst):
        res = lax.dot_general(src[0], unit, TN, preferred_element_type=F32)
        for p in range(NX):
            low = res[p * chip:p * chip + feat]
            high = res[p * chip + feat:(p + 1) * chip]
            dst[p, 0] = jnp.where(c == 0, low, high).astype(BF)
            dst[p, 1] = jnp.where(c == 0, high, low).astype(BF)

    def cut_up(n, src):
        for p in range(NX):
            w_cut[n, p] = src[0, :, p * chip:(p + 1) * chip]

    transpose(w_gate, t_gate)
    cut_up(0, w_gate)
    n_in = 2 * n_slot
    q_out, q_in = iota((n_in, n_in), 0), iota((n_in, n_in), 1)
    per = NZ * CAP
    want = ((q_out % per) // CAP) * (4 * CAP) + (q_out // per) * CAP + q_out % CAP
    perm = jnp.where(q_in == want, 1.0, 0.0).astype(BF)

    def regroup(copies, src, dst):
        for copy in copies:
            copy.wait_recv()
        moved = lax.dot_general(perm, src[...].reshape(n_in, WIDE), NN, preferred_element_type=F32)
        dst[...] = moved.astype(BF).reshape(dst.shape)

    regroup(z_copies, z_in, y_out)

    def spread(src, dst, send, recv):
        copies = {}
        for i in (1, 3, 2, 0, 4, 5, 7, 6):
            hh, yv = y_of(i)
            for o in range(2):
                if i == 0 and o == 0:
                    continue
                cc = (c + o) % 2
                copies[i, o] = remote(
                    src.at[hh, cc], dst.at[c, (i // HALF) * HALF + yy],
                    send.at[i, o], recv.at[i, o], at(z, hh * HALF + yv, x, cc),
                )
        dst[c, yy] = src[h, c]
        return copies

    y_copies = spread(y_out, y_in, ys, yr)
    transpose(w_up, t_up)
    cut_up(1, w_up)
    cut_up(2, w_down)
    f_copy.wait_recv()
    h_copies = to_z(f_out, h_in, hs, hr)

    right, left = (x + 1) % NX, (x + NX - 1) % NX
    g_copies, b_copies = {}, {}

    def target(way, dist):
        return (x + dist) % NX if way == 0 else (x + NX - dist) % NX

    def cut(parts, n):
        lo = sum(parts[:n])
        return pl.ds(lo, parts[n])

    def hand_over(j, n, p, m):
        rest = acts.at[c, j, p, cut(G_CUT, m)]
        b_copies[j, n, m] = remote(rest, rest, bs.at[j, n, m], br.at[j, n, m], at(z, y, x, 1 - c))

    def forward(j, way, s, m):
        piece = acts.at[c, j, target(1 - way, s), cut(G_CUT, m)]
        g_copies[j, way, s, m] = remote(
            piece, piece, gs.at[j, way, s, m], gr.at[j, way, s, m],
            at(z, y, right if way == 0 else left, c),
        )

    def prepare(j, copies, src, p):
        for i in range(j * HALF, j * HALF + HALF):
            for o in range(2):
                if (i, o) in copies:
                    copies[i, o].wait_recv()
        halves = []
        for core in range(2):
            block = src[core, j * HALF:(j + 1) * HALF].reshape(LANES, WIDE)
            halves.append(block.astype(F32).T[:feat])
        acts[c, j, p] = jnp.concatenate(halves, axis=0).astype(BF)

    def begin(j):
        for m in range(len(G_CUT)):
            forward(j, 0, 0, m)
            forward(j, 1, 0, m)
        for m in range(len(G_CUT)):
            hand_over(j, 0, x, m)

    def arrive(j, s):
        for m in range(len(G_CUT)):
            for way in range(2):
                g_copies[j, way, s - 1, m].wait_recv()
                if s < STEPS:
                    forward(j, way, s, m)
                hand_over(j, s if way == 0 else STEPS + s, target(1 - way, s), m)

    def add_piece(n, p, first=False):
        for j in range(2):
            for m in range(len(G_CUT)):
                b_copies[j, n, m].wait_recv()
        for n, a in ((0, 0), (1, 0), (2, 1)):
            piece = jnp.concatenate([acts[a, 0, p], acts[a, 1, p]], axis=1)
            res = lax.dot_general(w_cut[n, p], piece, NN, preferred_element_type=F32)
            pre[n] = res if first else pre[n] + res

    def add_step(s):
        add_piece(s, target(1, s))
        add_piece(STEPS + s, target(0, s))

    def gradients():
        gate, up, down = pre[0], pre[1], pre[2]
        sig = 1.0 / (1.0 + jnp.exp(-gate))
        up_grad = (down * gate * sig).astype(BF)
        gate_grad = (down * up * sig * (1.0 + gate * (1.0 - sig))).astype(BF)
        return gate_grad, up_grad

    p_copies = {}

    def partials(gate_grad, up_grad):
        fill = jnp.zeros((rows - feat, LANES), F32)
        for n, (way, dist) in enumerate(ORDER):
            d = target(way, dist)
            for side in range(2):
                res = lax.dot_general(t_gate[d, side], gate_grad, NN, preferred_element_type=F32)
                res += lax.dot_general(t_up[d, side], up_grad, NN, preferred_element_type=F32)
                for j in range(2):
                    here = jnp.concatenate([res[:, j * LANES:(j + 1) * LANES], fill], axis=0)
                    if side == 0:
                        keep[d, j] = here
                    else:
                        part[d, j] = here.astype(BF)
            p_copies[way, dist] = remote(
                part.at[d], twin.at[d], ps.at[n], pr.at[n], at(z, y, x, 1 - c)
            )

    met = set()

    def own(j, way, dist):
        key = (0, 0) if dist == 0 else (way, dist)
        if key not in met:
            met.add(key)
            p_copies[key].wait_recv()
        d = target(way, dist)
        return keep[d, j] + twin[d, j].astype(F32)

    c_copies = {}

    def link(j, way, t):
        val = own(j, way, STEPS - t)
        for m in range(len(C_CUT)):
            here = cut(C_CUT, m)
            lo, hi = sum(C_CUT[:m]), sum(C_CUT[:m + 1])
            send = val[lo:hi]
            if t > 0:
                c_copies[j, way, t - 1, m].wait_recv()
                send += chain_in[j, way, t - 1, lo:hi].astype(F32)
            chain_out[j, way, t, lo:hi] = send.astype(BF)
            c_copies[j, way, t, m] = remote(
                chain_out.at[j, way, t, here], chain_in.at[j, way, t, here],
                cs.at[j, way, t, m], cr.at[j, way, t, m],
                at(z, y, right if way == 0 else left, c),
            )

    def give_back(j, val, src, dst, send, recv, copies):
        val = jnp.concatenate([val, jnp.zeros((WIDE - rows, LANES), F32)], axis=0)
        src[j] = val.T.astype(BF).reshape(src.shape[1:])
        for i in ((1, 3, 2), (4, 5, 7, 6))[j]:
            hh, yv = y_of(i)
            copies[i] = remote(
                src.at[j, yv], dst.at[j * HALF + yy], send.at[i], recv.at[i],
                at(z, hh * HALF + yv, x, c),
            )
        if j == 0:
            dst[yy] = src[0, yy]

    def collect(src, copies):
        sums = []
        for j in range(2):
            for i in range(j * HALF, j * HALF + HALF):
                if i > 0:
                    copies[i].wait_recv()
            total = src[j * HALF].astype(F32)
            for n in range(1, HALF):
                total += src[j * HALF + n].astype(F32)
            sums.append(total)
        return jnp.concatenate(sums, axis=0)

    for j in range(2):
        prepare(j, y_copies, y_in, x)
        begin(j)
    drain(len(z_copies) + 1 + len(y_copies))
    regroup(h_copies, h_in, h_out)
    f_copies = spread(h_out, f_in, ws, wr)
    for s in range(1, STEPS + 1):
        for j in range(2):
            arrive(j, s)
        if s == 1:
            add_piece(0, x, True)
        elif s == 2:
            drain(len(h_copies))
            add_step(1)
            for j in range(2):
                prepare(j, f_copies, f_in, opposite)
                for m in range(len(G_CUT)):
                    hand_over(j, NX - 1, opposite, m)
    add_step(2)
    add_piece(NX - 1, opposite)
    add_step(STEPS)
    partials(*gradients())
    k_copies = {}
    for t in range(STEPS):
        if t == 2:
            drain()
        if t == 1:
            for j in (1, 0):
                give_back(j, own(j, 0, FAR), far_out, far_in, ks, kr, k_copies)
        for j in (1, 0):
            link(j, j, t)
            link(j, 1 - j, t)
    sum_out[...] = collect(far_in, k_copies).astype(BF)
    e_copy = remote(sum_out, sum_in, es.at[0], er.at[0], at(z, y, opposite, c))
    u_copies = {}
    for j in (1, 0):
        val = own(j, 0, 0)
        for way in range(2):
            for m in range(len(C_CUT)):
                c_copies[j, way, STEPS - 1, m].wait_recv()
            val += chain_in[j, way, STEPS - 1].astype(F32)
        give_back(j, val, back_out, back_in, us, ur, u_copies)
    both = collect(back_in, u_copies)
    e_copy.wait_recv()
    both += sum_in[...].astype(F32)

    v_out, v_in = iota((n_slot, n_slot), 0), iota((n_slot, n_slot), 1)
    half = (v_out // CAP) % 2
    rel = (half + h) % 2
    src = rel * per + (v_out // (2 * CAP)) * CAP + v_out % CAP
    turn = jnp.where(v_in == src, 1.0, 0.0)
    last_out[...] = lax.dot_general(
        turn, both, NN, precision=lax.Precision.HIGHEST, preferred_element_type=F32
    ).reshape(last_out.shape)
    v_copies = to_z(last_out, last_in, vs, vr)
    drain(len(started) - len(v_copies))
    pick = jnp.where(slot_col == iota((n_tok, n_slot), 1).astype(F32), 1.0, 0.0)
    for copy in v_copies:
        copy.wait_recv()
    got = lax.dot_general(
        pick, last_in[...].reshape(n_slot, WIDE), NN,
        precision=lax.Precision.HIGHEST, preferred_element_type=F32,
    )
    out[...] = (w_col * got[:, :feat]).astype(BF)

    drain()


def per_device(tokens, grad_out, route_weight, routes, gate_weight, up_weight, down_weight):
    n_tok, feat = tokens.shape
    _, hid, width = gate_weight.shape
    rows = -(-feat // 16) * 16
    vmem = pl.BlockSpec(memory_space=pltpu.VMEM)
    hbm = pl.BlockSpec(memory_space=pl.ANY)
    dma = pltpu.SemaphoreType.DMA
    n_slot = NZ * 2 * CAP
    return pl.pallas_call(
        kernel,
        out_shape=jax.ShapeDtypeStruct((n_tok, feat), BF),
        in_specs=[hbm] * 7,
        out_specs=vmem,
        scratch_shapes=[
            pltpu.VMEM((n_tok, feat), BF),
            pltpu.VMEM((n_tok, feat), BF),
            pltpu.VMEM((1, n_tok), F32),
            pltpu.VMEM((1, n_tok), jnp.int32),
            pltpu.VMEM((1, hid, width), BF),
            pltpu.VMEM((1, hid, width), BF),
            pltpu.VMEM((1, hid, width), BF),
            dma((7,)),
            pltpu.VMEM((NX, 2, feat, hid), BF),
            pltpu.VMEM((NX, 2, feat, hid), BF),
            pltpu.VMEM((3, NX, hid, 2 * feat), BF),
            pltpu.VMEM((3, hid, 2 * LANES), F32),
            pltpu.VMEM((NZ, 4 * CAP, WIDE), BF),
            pltpu.VMEM((NZ, 4 * CAP, WIDE), BF),
            pltpu.VMEM((2, 2, NZ * CAP, WIDE), BF),
            pltpu.VMEM((2, NY, NZ * CAP, WIDE), BF),
            pltpu.VMEM((NZ, 4 * CAP, WIDE), BF),
            pltpu.VMEM((NZ, 4 * CAP, WIDE), BF),
            pltpu.VMEM((2, 2, NZ * CAP, WIDE), BF),
            pltpu.VMEM((2, NY, NZ * CAP, WIDE), BF),
            pltpu.VMEM((2, 2, NX, 2 * feat, LANES), BF),
            pltpu.VMEM((NX, 2, rows, LANES), F32),
            pltpu.VMEM((NX, 2, rows, LANES), BF),
            pltpu.VMEM((NX, 2, rows, LANES), BF),
            pltpu.VMEM((2, 2, STEPS, rows, LANES), BF),
            pltpu.VMEM((2, 2, STEPS, rows, LANES), BF),
            pltpu.VMEM((2, HALF, NZ * CAP, WIDE), BF),
            pltpu.VMEM((NY, NZ * CAP, WIDE), BF),
            pltpu.VMEM((2, HALF, NZ * CAP, WIDE), BF),
            pltpu.VMEM((NY, NZ * CAP, WIDE), BF),
            pltpu.VMEM((2 * NZ * CAP, WIDE), BF),
            pltpu.VMEM((2 * NZ * CAP, WIDE), BF),
            pltpu.VMEM((NZ, 2 * CAP, WIDE), F32),
            pltpu.VMEM((NZ, 2 * CAP, WIDE), F32),
            dma((NZ - 1,)), dma((NZ - 1,)),
            dma((NY, 2)), dma((NY, 2)),
            dma((1,)), dma((1,)),
            dma((NZ - 1,)), dma((NZ - 1,)),
            dma((NY, 2)), dma((NY, 2)),
            dma((2, 2, STEPS, 2)), dma((2, 2, STEPS, 2)),
            dma((2, NX, 2)), dma((2, NX, 2)),
            dma((NX,)), dma((NX,)),
            dma((2, 2, STEPS, 2)), dma((2, 2, STEPS, 2)),
            dma((NY,)), dma((NY,)),
            dma((NY,)), dma((NY,)),
            dma((1,)), dma((1,)),
            dma((NZ - 1,)), dma((NZ - 1,)),
        ],
        compiler_params=pltpu.CompilerParams(
            collective_id=0, has_side_effects=True, vmem_limit_bytes=60 * 1024 * 1024
        ),
    )(
        tokens, grad_out, route_weight.reshape(1, n_tok), routes.reshape(1, n_tok),
        gate_weight, up_weight, down_weight,
    )


def solution(mesh):
    return jax.shard_map(
        per_device,
        mesh=mesh,
        in_specs=(
            P("ep", "tp"),
            P("ep", "tp"),
            P("ep"),
            P("ep", None),
            P("ep", "tp", None),
            P("ep", "tp", None),
            P("ep", "tp", None),
        ),
        out_specs=P("ep", "tp"),
        check_vma=False,
    )
```
